32 devices in a mesh: groups: 2 (over y), rows: 16 (over z, x, core).
Axes of the slice: x: 2, y: 2, z: 4, core: 2. Of those that a mesh axis runs over, the one named last changes fastest.
Arguments:
- atmos: float32 [3, 4, 256, 1024], P(None, None, ('groups', 'rows')), parts along dimension 2, may hold values from -4 to 4
- level_set: float32 [1024, 4096], P(('groups', 'rows')), parts along dimension 0, may hold values from -8 to 8
- fuel: int32 [1024, 4096], P(('groups', 'rows')), parts along dimension 0, may hold values from 0 to 12
- fuel_table: float32 [3, 13], replicated, may hold values from 0.2 to 1
- band_home: int32 [1024, 1], P(('groups', 'rows')), parts along dimension 0, may hold values from 0 to 15; in each aligned block of 32 rows (0 to 31, 32 to 63, ...) at most 4 rows name the same one
- band_tile: int32 [1024], P(('groups', 'rows')), parts along dimension 0, may hold values from 0 to 511
Outputs:
- new_level_set: float32 [1024, 4096], P(('groups', 'rows')), parts along dimension 0
- new_atmos: float32 [3, 4, 256, 1024], P(None, None, ('groups', 'rows')), parts along dimension 2
The draws below stay inside these ranges and needn't reach their ends.
There are 2 independent parts, one for each index of `groups`. The reference program is written for one: setup_inputs(seed, part) draws one part's arguments, and reference() takes and returns one part's arrays. A program takes and returns all parts, laid end to end along the dimension named above; an argument that names none is the same for every part. Nothing has to cross between parts.
Inputs may be any that keep to these rules, and one draw needn't show every extreme that they name: `band_home`: among the tiles listed on one device, at most 4 share one home block. `band_tile`: tile indices may repeat; repeated tiles add their heating.
All inputs are finite; a program needn't handle non-finite values.
Results may differ from the reference program's by a relative error of at most 0.0003.
Values sent between devices are 32-bit elements; how exact they have to be, the bound alone decides.
A program may use at most 192 MiB of HBM per device.

```python
import math
import jax
import jax.numpy as jnp
import numpy as np
from jax import lax

TILE = 64
REFINE = 16
CPT = 4
CELLS = 4096
SUBSTEPS = 4
LEV = 4
NFUEL = 13
AROWS = 8
NC = 1024
SLOTS = 32
OWNERS = 16
CAP = 4
BAND = 512
NR = 128
TPD = 512


def with_ends(values, key, low, largest):
    longest = values.shape.index(max(values.shape))
    spots = []
    for shift in (0, 1):
        where = [jax.random.randint(jax.random.fold_in(key, axis), (), 0, length) for axis, length in enumerate(values.shape)]
        where[longest] = (where[longest] + shift) % values.shape[longest]
        spots.append(tuple(where))
    return values.at[spots[0]].set(low).at[spots[1]].set(largest)


def level_of(stream_key, dims, pieces, smallest, high):
    loudness, own = 1.0, jax.random.fold_in(stream_key, 6)
    for position, blocks in pieces:
        heights = jnp.exp(jax.random.uniform(jax.random.fold_in(own, position), (blocks,), jnp.float32, smallest / len(pieces), high / len(pieces)))
        loudness = loudness * jnp.repeat(heights, dims[position] // blocks).reshape([-1 if axis == position else 1 for axis in range(len(dims))])
    return loudness


def routed_block(stream_key, own, number, rows, number_of, top, bound, skew):
    ranking = jax.random.permutation(stream_key, number_of)
    heavy_load, common = portions_of(number_of, rows * top, bound, skew, True), portions_of(number_of, rows * top, bound, skew, False)
    places = jnp.arange(number_of)

    def named(tallies, turn):
        used = int((tallies > 0).sum())
        fixed = max(1, used // 4)
        moved = fixed + (places - fixed + turn * (used - fixed)) % max(1, number_of - fixed)
        return jnp.zeros((number_of,), jnp.int32).at[ranking[jnp.where(places < fixed, places, moved)]].set(jnp.asarray(tallies, jnp.int32))

    tallies = jnp.where(number % 4 == 0, named(heavy_load, number // 4), named(common, number - number // 4 - 1))
    mixed = jax.random.permutation(jax.random.fold_in(own, 3), number_of)
    donor, taker = mixed[0:number_of // 2 * 2:2], mixed[1:number_of // 2 * 2:2]
    slack = jnp.minimum(tallies[donor] - 1, bound - tallies[taker]) // 2
    slack = jnp.where((donor == ranking[0]) | (taker == ranking[0]) | (tallies[taker] == 0), 0, jnp.maximum(slack, 0))
    moved = jax.random.randint(jax.random.fold_in(own, 4), (number_of // 2,), 0, 1 << 20) % (slack + 1)
    tallies = tallies.at[donor].add(-moved).at[taker].add(moved)
    items = jnp.searchsorted(jnp.cumsum(tallies), jnp.arange(rows * top), side="right").astype(jnp.int32)
    grid = items.reshape(top, rows).T
    grid = grid[jax.random.permutation(jax.random.fold_in(own, 1), rows)]
    turn = jax.random.randint(jax.random.fold_in(own, 2), (rows, 1), 0, top)
    return jnp.take_along_axis(grid, (jnp.arange(top)[None, :] + turn) % top, axis=1)


def portions_of(number_of, total, most, skew, full):
    portions = [(1 << 20) // math.isqrt(standing ** skew) + 1 for standing in range(1, number_of + 1)]
    largest = most if full else min(most, max(-(-total // number_of), total * portions[0] // sum(portions)))
    least = 1 if total - largest >= number_of - 1 else 0
    given, spare = [largest] + [least] * (number_of - 1), total - largest - least * (number_of - 1)
    while spare > 0:
        candidates = [i for i in range(1, number_of) if given[i] < largest] or [i for i in range(1, number_of) if given[i] < most]
        pool, remaining = sum([portions[i] for i in candidates]), spare
        for i in candidates:
            extra = min(most - given[i], max(1, remaining * portions[i] // pool), spare)
            given[i] = given[i] + extra
            spare = spare - extra
    return np.array(given)


def gaussian(own_key, dims, spread, limit, cuts=(), kind=jnp.bfloat16):
    entries = jax.random.normal(own_key, dims, jnp.float32) * spread
    if len(cuts) > 0:
        entries = level_of(own_key, dims, cuts, -0.22, 0.18) * entries
    return jnp.clip(entries, min=-limit, max=limit).astype(kind)


def setup_inputs(seed: int = 0, part: int = 0) -> dict:
    splits = jax.random.split(jax.random.key(seed), 7)
    part_keys = jax.random.split(jax.random.fold_in(splits[6], part), 7)
    atmos = gaussian(part_keys[0], (3, LEV, NR, NC), 1.0, 4.0, ((2, 16),), jnp.float32)
    level_set = gaussian(part_keys[1], (BAND, CELLS), 2.0, 8.0, ((0, 16),), jnp.float32)
    fuel = with_ends(jax.random.randint(part_keys[2], (BAND, CELLS), 0, NFUEL), jax.random.fold_in(part_keys[2], 1), 0, NFUEL - 1).astype(jnp.int32)
    fuel_table = jnp.clip(jax.random.uniform(splits[3], (3, NFUEL), jnp.float32, 0.2, 1.0), 0.2, 1.0)
    band_home_keys = jax.random.split(jax.random.fold_in(part_keys[4], 1), BAND // SLOTS)
    band_home_turns = jax.random.permutation(jax.random.fold_in(part_keys[4], 3), BAND // SLOTS)
    band_home = jax.vmap(lambda own, number: routed_block(jax.random.fold_in(part_keys[4], 2), own, number, SLOTS, OWNERS, 1, CAP, 3))(band_home_keys, band_home_turns).reshape((BAND, 1))
    band_tile = with_ends(jax.random.randint(part_keys[5], (BAND,), 0, TPD), jax.random.fold_in(part_keys[5], 1), 0, TPD - 1).astype(jnp.int32)
    return {"atmos": atmos, "level_set": level_set, "fuel": fuel, "fuel_table": fuel_table, "band_home": band_home, "band_tile": band_tile}


fire_step = 0.1
air_step = 0.1
spread_floor = 0.01
viscosity = 0.5
mixing = 0.5
coupling = 1.0

def weight_table():
    spots = (np.arange(TILE) + 0.5) / REFINE + 0.5
    nodes = np.arange(CPT + 2)
    return np.maximum(0.0, 1.0 - np.abs(spots[:, None] - nodes[None, :]))

def fine_wind(patches):
    table = jnp.asarray(weight_table(), dtype=jnp.float32)
    return jnp.einsum('ap,ncpq,bq->ncab', table, patches, table, precision=lax.Precision.HIGHEST)

def fuel_params(fuel_cells, fuel_table):
    count_tiles = fuel_cells.shape[0]
    params = jnp.zeros((3, count_tiles, CELLS), jnp.float32)
    for kind in range(NFUEL):
        params = jnp.where((fuel_cells == kind)[None], fuel_table[:, kind][:, None, None], params)
    return params.reshape(3, count_tiles, TILE, TILE)

def sides(values, axis):
    size = values.shape[axis]
    nexts = jnp.concatenate([lax.slice_in_dim(values, 1, size, axis=axis), lax.slice_in_dim(values, size - 1, size, axis=axis)], axis=axis)
    prevs = jnp.concatenate([lax.slice_in_dim(values, 0, 1, axis=axis), lax.slice_in_dim(values, 0, size - 1, axis=axis)], axis=axis)
    return (values - prevs, nexts - values)

def burn(level, surface_wind, params):
    rate, reach, warmth = (params[0], params[1], params[2])
    flow_rows = reach * surface_wind[:, 0]
    flow_cols = reach * surface_wind[:, 1]
    flux = jnp.zeros_like(level)
    for step in range(SUBSTEPS):
        back_rows, ahead_rows = sides(level, 1)
        back_cols, ahead_cols = sides(level, 2)
        slope = jnp.maximum(back_rows, 0.0) ** 2 + jnp.minimum(ahead_rows, 0.0) ** 2
        slope = slope + jnp.maximum(back_cols, 0.0) ** 2 + jnp.minimum(ahead_cols, 0.0) ** 2
        moving = jnp.maximum(flow_rows, 0.0) * back_rows + jnp.minimum(flow_rows, 0.0) * ahead_rows
        moving = moving + jnp.maximum(flow_cols, 0.0) * back_cols + jnp.minimum(flow_cols, 0.0) * ahead_cols
        level = level - fire_step * (rate * jnp.sqrt(slope + spread_floor) + moving)
        flux = flux + warmth * jnp.exp(-level * level)
    return (level, flux / SUBSTEPS)

def coarse_heat(flux):
    count_tiles = flux.shape[0]
    summed = flux.reshape(count_tiles, CPT, REFINE, CPT, REFINE).sum(axis=(2, 4))
    return summed.reshape(count_tiles, CPT * CPT) / (REFINE * REFINE)

def advance(padded, heating):
    full = jnp.pad(padded, ((0, 0), (0, 0), (0, 0), (1, 1)))
    centre = full[:, :, 1:-1, 1:-1]
    north = full[:, :, :-2, 1:-1]
    south = full[:, :, 2:, 1:-1]
    west = full[:, :, 1:-1, :-2]
    east = full[:, :, 1:-1, 2:]
    laplace = north + south + west + east - 4.0 * centre
    above = jnp.concatenate([centre[:, 1:], centre[:, -1:]], axis=1)
    below = jnp.concatenate([centre[:, :1], centre[:, :-1]], axis=1)
    vertical = above + below - 2.0 * centre
    carried = centre[0:1] * (south - north) * 0.5 + centre[1:2] * (east - west) * 0.5
    updated = centre + air_step * (viscosity * laplace + mixing * vertical - carried)
    return updated.at[2, 0].add(coupling * heating)

def reference(atmos, level_set, fuel, fuel_table, band_home, band_tile):
    across = NC // CPT
    tiles_dev = AROWS // CPT * across
    padded = jnp.pad(atmos, ((0, 0), (0, 0), (1, 1), (0, 0)))
    surface = jnp.pad(padded[:2, 0], ((0, 0), (0, 0), (1, 1)))
    owner_of = band_home[:, 0].astype(jnp.int32)
    row_start = (owner_of * AROWS + band_tile // across * CPT).astype(jnp.int32)
    col_start = (band_tile % across * CPT).astype(jnp.int32)
    anchor = jnp.zeros((), jnp.int32)
    patches = jax.vmap(lambda r, c: lax.dynamic_slice(surface, (anchor, r, c), (2, CPT + 2, CPT + 2)))(row_start, col_start)
    blocks = BAND // SLOTS

    def one_block(item):
        block_level, block_fuel, block_patch = item
        winds = fine_wind(block_patch)
        params = fuel_params(block_fuel, fuel_table)
        stepped, flux = burn(block_level.reshape(SLOTS, TILE, TILE), winds, params)
        return (stepped.reshape(SLOTS, CELLS), coarse_heat(flux))
    stepped, coarse = lax.map(one_block, (level_set.reshape(blocks, SLOTS, CELLS), fuel.reshape(blocks, SLOTS, CELLS), patches.reshape(blocks, SLOTS, 2, CPT + 2, CPT + 2)))
    global_tile = (owner_of * tiles_dev + band_tile).astype(jnp.int32)
    heat_tiles = jnp.zeros((OWNERS * tiles_dev, CPT * CPT), jnp.float32).at[global_tile].add(coarse.reshape(BAND, CPT * CPT))
    heating = heat_tiles.reshape(OWNERS * (AROWS // CPT), across, CPT, CPT).transpose(0, 2, 1, 3).reshape(NR, NC)
    return (stepped.reshape(BAND, CELLS), advance(padded, heating))
```

```python
import functools

import jax
import jax.numpy as jnp
import ml_dtypes
import numpy as np
from jax import lax
from jax.experimental import pallas as pl
from jax.experimental.pallas import tpu as pltpu
from jax.sharding import PartitionSpec as P

TILE = 64
REFINE = 16
CPT = 4
CELLS = 4096
SUBSTEPS = 4
NFUEL = 13
ROWS8 = 8
LANES = 128
SPAN = CPT + 2
PIECE = 40

fire_step = 0.1
air_step = 0.1
spread_floor = 0.01
viscosity = 0.5
mixing = 0.5
coupling = 1.0

F32 = jnp.float32
BF16 = jnp.bfloat16
HIGHEST = lax.Precision.HIGHEST


def weight_table():
    spots = (np.arange(TILE) + 0.5) / REFINE + 0.5
    nodes = np.arange(SPAN)
    return np.maximum(0.0, 1.0 - np.abs(spots[:, None] - nodes[None, :]))


def spread_weights():
    table = weight_table()
    both = np.einsum("ap,bq->qpab", table, table).reshape(SPAN * SPAN, CELLS).astype(np.float32)
    high = both.astype(ml_dtypes.bfloat16)
    low = (both - high.astype(np.float32)).astype(ml_dtypes.bfloat16)
    out = np.zeros((LANES, CELLS), ml_dtypes.bfloat16)
    for place, part in enumerate((high, high, low)):
        out[place * PIECE : place * PIECE + SPAN * SPAN] = part
    return out


def iota(shape, dim):
    return lax.broadcasted_iota(jnp.int32, shape, dim)


def halves(x):
    high = x.astype(BF16)
    return high, (x - high.astype(F32)).astype(BF16)


def dot(a, b):
    return jnp.dot(a, b, preferred_element_type=F32)


def dot_nt(a, b, precision=None):
    return lax.dot_general(
        a, b, (((1,), (1,)), ((), ())), preferred_element_type=F32, precision=precision
    )


def kernel(
    n,
    home_ref,
    tile_ref,
    table_ref,
    kron_hbm,
    atmos_hbm,
    level_hbm,
    fuel_hbm,
    newlev_hbm,
    newatm_hbm,
    kron,
    atmos,
    newatm,
    phi,
    fuel,
    rate,
    flow_r,
    flow_c,
    warm,
    acc,
    winds,
    patches,
    land,
    edge_a,
    rim_a,
    edge_b,
    rim_b,
    req,
    want,
    pick,
    back,
    heat,
    got,
    load_sem,
    save_sem,
    edge_send,
    rim_recv,
    all_send,
    all_recv,
):
    me = lax.axis_index("rows")
    slots = phi.shape[1]
    fields, levels, arows, ncols = atmos.shape
    strips = arows // CPT
    across = ncols // CPT
    cap = max(2, 2 * slots // n)
    nk = n * ROWS8

    loads = [
        pltpu.make_async_copy(src, dst, load_sem.at[i])
        for i, (src, dst) in enumerate(
            (
                (atmos_hbm, atmos),
                (fuel_hbm, fuel),
                (level_hbm, phi.at[0]),
                (kron_hbm, kron),
            )
        )
    ]
    for load in loads:
        load.start()

    rim_a[...] = jnp.zeros_like(rim_a)
    rim_b[...] = jnp.zeros_like(rim_b)

    barrier = pltpu.get_barrier_semaphore()

    def greet(d, c):
        pl.semaphore_signal(
            barrier,
            inc=1,
            device_id={"rows": lax.rem(me + d, n)},
            device_id_type=pl.DeviceIdType.MESH,
        )
        return c

    lax.fori_loop(1, n, greet, 0)

    eye = iota((slots, slots), 0) == iota((slots, slots), 1)
    earlier = iota((slots, slots), 0) < iota((slots, slots), 1)
    home_row = home_ref[...].astype(F32)
    tile_row = tile_ref[...].astype(F32)
    home_col = jnp.sum(jnp.where(eye, home_row, 0.0), axis=1, keepdims=True)
    same = (home_col == home_row) & earlier
    rank_row = jnp.sum(jnp.where(same, 1.0, 0.0), axis=0, keepdims=True)
    place_row = home_row * ROWS8 + rank_row
    place_col = jnp.sum(jnp.where(eye, place_row, 0.0), axis=1, keepdims=True)
    placing_t = iota((nk, slots), 0).astype(F32) == place_row
    placing = jnp.where(place_col == iota((slots, nk), 1).astype(F32), 1.0, 0.0).astype(BF16)
    asked = jnp.sum(jnp.where(placing_t, tile_row, 0.0), axis=1, keepdims=True)
    req[...] = jnp.broadcast_to(asked, (nk, LANES))

    loads[0].wait()
    for side, row in ((0, arows - 1), (1, 0)):
        for f in range(2):
            edge_a[side, f : f + 1, :] = atmos[f, 0, row : row + 1, :]
        for f in range(fields):
            for k in range(levels):
                at = f * levels + k
                edge_b[side, at : at + 1, :] = atmos[f, k, row : row + 1, :]

    pl.semaphore_wait(barrier, n - 1)

    def edge_copy(side, which):
        src, dst = ((edge_a, rim_a), (edge_b, rim_b))[which]
        return pltpu.make_async_remote_copy(
            src_ref=src.at[side],
            dst_ref=dst.at[side],
            send_sem=edge_send.at[which, side],
            recv_sem=rim_recv.at[which, side],
            device_id={"rows": jnp.clip(me + (1 - 2 * side), 0, n - 1)},
            device_id_type=pl.DeviceIdType.MESH,
        )

    def send_edges(which):
        @pl.when(me < n - 1)
        def _():
            edge_copy(0, which).start()

        @pl.when(me > 0)
        def _():
            edge_copy(1, which).start()

    def recv_edges(which):
        @pl.when(me > 0)
        def _():
            edge_copy(0, which).wait_recv()

        @pl.when(me < n - 1)
        def _():
            edge_copy(1, which).wait_recv()

    def sent_edges(which):
        @pl.when(me < n - 1)
        def _():
            edge_copy(0, which).wait_send()

        @pl.when(me > 0)
        def _():
            edge_copy(1, which).wait_send()

    mine = pl.ds(pl.multiple_of(me * ROWS8, ROWS8), ROWS8)

    def exchange(src, dst, number):
        def send(d, c):
            peer = lax.rem(me + d, n)
            pltpu.make_async_remote_copy(
                src_ref=src.at[pl.ds(pl.multiple_of(peer * ROWS8, ROWS8), ROWS8)],
                dst_ref=dst.at[mine],
                send_sem=all_send.at[number],
                recv_sem=all_recv.at[number],
                device_id={"rows": peer},
                device_id_type=pl.DeviceIdType.MESH,
            ).start()
            return c

        lax.fori_loop(1, n, send, 0)

    def arrive(src, dst, number):
        others = pl.ds(0, (n - 1) * ROWS8)
        pltpu.make_async_copy(dst.at[others], dst.at[others], all_recv.at[number]).wait()
        dst[mine, :] = src[mine, :]

    def gone(src, number):
        others = pl.ds(0, (n - 1) * ROWS8)
        pltpu.make_async_copy(src.at[others], src.at[others], all_send.at[number]).wait()

    send_edges(0)
    exchange(req, want, 0)
    send_edges(1)

    loads[1].wait()

    def params(v, c):
        cols = pl.ds(pl.multiple_of(v * LANES, LANES), LANES)
        kinds = fuel[:, cols]
        bits = [(kinds & (1 << b)) != 0 for b in range(4)]
        for row, (ref, scale) in enumerate(((rate, fire_step), (flow_r, fire_step), (warm, 1.0))):
            vals = [table_ref[row, i] * scale for i in range(NFUEL)]
            for bit in bits:
                nxt = []
                for i in range(0, len(vals), 2):
                    if i + 1 < len(vals):
                        nxt.append(jnp.where(bit, vals[i + 1], vals[i]))
                    else:
                        nxt.append(vals[i])
                vals = nxt
            ref[:, cols] = vals[0]
        acc[:, cols] = jnp.zeros((slots, LANES), F32)
        return c

    lax.fori_loop(0, CELLS // LANES, params, 0)

    recv_edges(0)
    for f in range(2):
        winds[f, 0:1, :] = rim_a[0, f : f + 1, :]
        winds[f, 1 : 1 + arows, :] = atmos[f, 0]
        winds[f, 1 + arows : 2 + arows, :] = rim_a[1, f : f + 1, :]
        winds[f, 2 + arows : 8 + arows, :] = jnp.zeros((6, ncols), F32)
    col8 = iota((ROWS8, ncols), 1)
    patches[...] = jnp.zeros_like(patches)
    for f in range(2):
        for strip in range(strips):
            base = winds[f, strip * CPT : strip * CPT + ROWS8, :]
            for q in range(SPAN):
                moved = base if q == 1 else pltpu.roll(base, (1 - q) % ncols, axis=1)
                if q == 0:
                    moved = jnp.where(col8 == 0, 0.0, moved)
                if q == SPAN - 1:
                    moved = jnp.where(col8 >= ncols - CPT, 0.0, moved)
                at = f * 64 + q * SPAN
                patches[at : at + SPAN, strip * ncols : (strip + 1) * ncols] = moved[:SPAN]
    table_high, table_low = halves(patches[...])

    arrive(req, want, 0)
    for chunk in range(0, nk, LANES):
        t = want[chunk : chunk + LANES, 0:1]
        hot = jnp.where(
            iota((LANES, strips * ncols), 1).astype(F32) == CPT * t, 1.0, 0.0
        ).astype(BF16)
        pick[chunk : chunk + LANES, :] = dot_nt(hot, table_high) + dot_nt(hot, table_low)
    exchange(pick, back, 1)

    for chunk in range(0, nk, LANES):
        t = want[chunk : chunk + LANES, 0:1]
        for strip in range(1, strips):
            t = jnp.where(t >= across, t - across, t)
        group = (iota((LANES, ncols), 1) // CPT).astype(F32)
        land[chunk : chunk + LANES, :] = jnp.where(group == t, 1.0, 0.0).astype(BF16)

    recv_edges(1)
    row8 = iota((arows, ncols), 0)
    colx = iota((arows, ncols), 1)
    for k in range(levels):
        wind_r = atmos[0, k] * (0.5 * air_step)
        wind_c = atmos[1, k] * (0.5 * air_step)
        for f in range(fields):
            at = f * levels + k
            centre = atmos[f, k]
            north = jnp.where(row8 == 0, rim_b[0, at : at + 1, :], pltpu.roll(centre, 1, axis=0))
            south = jnp.where(
                row8 == arows - 1, rim_b[1, at : at + 1, :], pltpu.roll(centre, arows - 1, axis=0)
            )
            west = jnp.where(colx == 0, 0.0, pltpu.roll(centre, 1, axis=1))
            east = jnp.where(colx == ncols - 1, 0.0, pltpu.roll(centre, ncols - 1, axis=1))
            above = atmos[f, min(k + 1, levels - 1)]
            below = atmos[f, max(k - 1, 0)]
            laplace = north + south + west + east - 4.0 * centre
            vertical = above + below - 2.0 * centre
            carried = wind_r * (south - north) + wind_c * (east - west)
            newatm[f, k] = (
                centre
                + (air_step * viscosity) * laplace
                + (air_step * mixing) * vertical
                - carried
            )

    loads[3].wait()
    arrive(pick, back, 1)
    back_high, back_low = halves(back[...])
    own_high = dot(placing, back_high)
    own_low = dot(placing, back_low)
    lane = iota((slots, LANES), 1)

    def field_rows(x):
        first = jnp.where(lane < 64, x, 0.0)
        second = jnp.where(lane < 64, pltpu.roll(x, 64, axis=1), 0.0)
        return jnp.concatenate([first, second], axis=0)

    high, low = field_rows(own_high), field_rows(own_low)
    left = (high + pltpu.roll(low, PIECE, axis=1) + pltpu.roll(high, 2 * PIECE, axis=1)).astype(
        BF16
    )

    def blow(v, c):
        cols = pl.ds(pl.multiple_of(v * 512, 512), 512)
        wind = dot(left, kron[:, cols])
        reach = flow_r[:, cols]
        flow_r[:, cols] = reach * wind[:slots]
        flow_c[:, cols] = reach * wind[slots:]
        return c

    lax.fori_loop(0, CELLS // 512, blow, 0)

    loads[2].wait()
    top_half = lane < TILE
    first_col = (lane & (TILE - 1)) == 0
    columns = CELLS // LANES

    def substep(step, c):
        now = lax.rem(step, 2)
        later = 1 - now

        def cell(v):
            return phi[now, :, v * LANES : (v + 1) * LANES]

        centre = cell(0)
        turned = pltpu.roll(centre, TILE, axis=1)
        before = centre
        for v in range(columns):
            cols = slice(v * LANES, (v + 1) * LANES)
            if v + 1 < columns:
                ahead = cell(v + 1)
                ahead_turned = pltpu.roll(ahead, TILE, axis=1)
            else:
                ahead, ahead_turned = None, centre
            prev = jnp.where(top_half, before, turned)
            nxt = jnp.where(top_half, turned, ahead_turned)
            back_r = centre - prev
            ahead_r = nxt - centre
            back_c = jnp.where(first_col, 0.0, centre - pltpu.roll(centre, 1, axis=1))
            ahead_c = pltpu.roll(back_c, LANES - 1, axis=1)
            a = jnp.maximum(back_r, 0.0)
            b = jnp.minimum(ahead_r, 0.0)
            d = jnp.maximum(back_c, 0.0)
            e = jnp.minimum(ahead_c, 0.0)
            slope = (a * a + b * b) + (d * d + e * e) + spread_floor
            fr = flow_r[:, cols]
            fc = flow_c[:, cols]
            move = fr * jnp.where(fr > 0.0, back_r, ahead_r) + fc * jnp.where(
                fc > 0.0, back_c, ahead_c
            )
            new = centre - (rate[:, cols] * (slope * lax.rsqrt(slope)) + move)
            phi[later, :, cols] = new
            acc[:, cols] += jnp.exp(-(new * new))
            before, centre, turned = turned, ahead, ahead_turned
        return c

    lax.fori_loop(0, SUBSTEPS, substep, 0)

    saves = [
        pltpu.make_async_copy(phi.at[0], newlev_hbm, save_sem.at[0]),
        pltpu.make_async_copy(newatm, newatm_hbm, save_sem.at[1]),
    ]
    saves[0].start()

    per = columns // CPT
    total = jnp.zeros((slots, LANES), F32)
    for i in range(CPT):
        part = jnp.zeros((slots, LANES), F32)
        for v in range(i * per, (i + 1) * per):
            cols = slice(v * LANES, (v + 1) * LANES)
            part = part + acc[:, cols] * warm[:, cols]
        source = iota((LANES, LANES), 0)
        target = iota((LANES, LANES), 1)
        mean = jnp.where(
            (source & (TILE - 1)) // REFINE + i * CPT == target,
            1.0 / (SUBSTEPS * REFINE * REFINE),
            0.0,
        ).astype(BF16)
        part_high, part_low = halves(part)
        total = total + dot(part_high, mean) + dot(part_low, mean)
    total_high, total_low = halves(total)
    out_of = jnp.where(placing_t, 1.0, 0.0).astype(BF16)
    heat[...] = dot(out_of, total_high) + dot(out_of, total_low)
    exchange(heat, got, 2)
    sent_edges(0)
    sent_edges(1)
    gone(req, 0)
    gone(pick, 1)
    arrive(heat, got, 2)

    spots = CPT * arows
    ranks = iota((spots, LANES), 0)
    r = ranks & (arows - 1)
    wanted_lane = (r // CPT) * (CPT * CPT) + (r % CPT) * CPT + ranks // arows
    choose = jnp.where(iota((spots, LANES), 1) == wanted_lane, 1.0, 0.0).astype(BF16)
    landed = jnp.zeros((2 * spots, ncols), F32)
    for chunk in range(0, nk, LANES):
        rows = slice(chunk, chunk + LANES)
        t = want[rows, :]
        x = got[rows, :]
        spread = jnp.zeros((LANES, LANES), F32)
        for strip in range(strips):
            here = (t >= strip * across) & (t < (strip + 1) * across)
            part = jnp.where(here, x, 0.0)
            if strip:
                part = pltpu.roll(part, strip * CPT * CPT, axis=1)
            spread = spread + part
        s_high, s_low = halves(spread)
        both = jnp.concatenate([dot_nt(choose, s_high), dot_nt(choose, s_low)], axis=0)
        landed = landed + dot(both.astype(BF16), land[rows, :])
    landed = landed[:spots] + landed[spots:]
    turn = colx & (CPT - 1)
    heating = landed[:arows]
    for j in range(1, CPT):
        heating = jnp.where(turn == j, landed[j * arows : (j + 1) * arows], heating)
    newatm[2, 0] = newatm[2, 0] + coupling * heating
    saves[1].start()
    gone(heat, 2)
    saves[0].wait()
    saves[1].wait()


def shards(n, atmos, level_set, fuel, fuel_table, band_home, band_tile):
    slots = level_set.shape[0]
    fields, levels, arows, ncols = atmos.shape
    nk = n * ROWS8
    cells = (slots, CELLS)
    vmem = pltpu.VMEM
    hbm = pl.BlockSpec(memory_space=pl.ANY)
    local = pl.BlockSpec(memory_space=pltpu.VMEM)
    kron = jnp.asarray(spread_weights())
    return pl.pallas_call(
        functools.partial(kernel, n),
        out_shape=(
            jax.ShapeDtypeStruct(level_set.shape, F32),
            jax.ShapeDtypeStruct(atmos.shape, F32),
        ),
        in_specs=[local, local, pl.BlockSpec(memory_space=pltpu.SMEM), hbm, hbm, hbm, hbm],
        out_specs=(hbm, hbm),
        scratch_shapes=[
            vmem((LANES, CELLS), BF16),
            vmem(atmos.shape, F32),
            vmem(atmos.shape, F32),
            vmem((2,) + cells, F32),
            vmem(cells, jnp.int32),
            vmem(cells, F32),
            vmem(cells, F32),
            vmem(cells, F32),
            vmem(cells, F32),
            vmem(cells, F32),
            vmem((2, arows + 8, ncols), F32),
            vmem((LANES, arows // CPT * ncols), F32),
            vmem((nk, ncols), BF16),
            vmem((2, 2, ncols), F32),
            vmem((2, 2, ncols), F32),
            vmem((2, fields * levels, ncols), F32),
            vmem((2, fields * levels, ncols), F32),
        ]
        + [vmem((nk, LANES), F32)] * 6
        + [
            pltpu.SemaphoreType.DMA((4,)),
            pltpu.SemaphoreType.DMA((2,)),
            pltpu.SemaphoreType.DMA((2, 2)),
            pltpu.SemaphoreType.DMA((2, 2)),
            pltpu.SemaphoreType.DMA((3,)),
            pltpu.SemaphoreType.DMA((3,)),
        ],
        compiler_params=pltpu.CompilerParams(
            collective_id=0, has_side_effects=True, vmem_limit_bytes=48 * 1024 * 1024
        ),
    )(
        band_home.reshape(1, slots),
        band_tile.reshape(1, slots),
        fuel_table,
        kron,
        atmos,
        level_set,
        fuel,
    )


def solution(mesh):
    placed = (
        P(None, None, ("groups", "rows"), None),
        P(("groups", "rows"), None),
        P(("groups", "rows"), None),
        P(),
        P(("groups", "rows"), None),
        P(("groups", "rows")),
    )
    return jax.shard_map(
        functools.partial(shards, mesh.shape["rows"]),
        mesh=mesh,
        in_specs=placed,
        out_specs=(P(("groups", "rows"), None), P(None, None, ("groups", "rows"), None)),
        check_vma=False,
    )
```

```python
import functools

import jax
import jax.numpy as jnp
import ml_dtypes
import numpy as np
from jax import lax
from jax.experimental import pallas as pl
from jax.experimental.pallas import tpu as pltpu
from jax.sharding import PartitionSpec as P

TILE = 64
REFINE = 16
CPT = 4
CELLS = 4096
SUBSTEPS = 4
NFUEL = 13
ROWS8 = 8
LANES = 128
SPAN = CPT + 2
PIECE = 40

fire_step = 0.1
air_step = 0.1
spread_floor = 0.01
viscosity = 0.5
mixing = 0.5
coupling = 1.0

F32 = jnp.float32
BF16 = jnp.bfloat16
HIGHEST = lax.Precision.HIGHEST


def weight_table():
    spots = (np.arange(TILE) + 0.5) / REFINE + 0.5
    nodes = np.arange(SPAN)
    return np.maximum(0.0, 1.0 - np.abs(spots[:, None] - nodes[None, :]))


def spread_weights():
    table = weight_table()
    out = np.zeros((2, LANES, SPAN, LANES), ml_dtypes.bfloat16)
    for half in range(2):
        for part in range(2):
            for q in range(SPAN):
                for p in range(SPAN):
                    at = part * PIECE + q * SPAN + p
                    out[half, at, p, half * TILE : (half + 1) * TILE] = table[:, q]
    return out.reshape(2 * LANES, SPAN * LANES)


def side_weights():
    out = np.zeros((2, LANES, 2, LANES), ml_dtypes.bfloat16)
    for b in range(LANES):
        if b % TILE:
            out[:, b, 0, b] = 1
            out[:, b - 1, 0, b] = -1
        if (b + 1) % TILE:
            out[:, b + 1, 1, b] = 1
            out[:, b, 1, b] = -1
    return out.reshape(2 * LANES, 2 * LANES)


def iota(shape, dim):
    return lax.broadcasted_iota(jnp.int32, shape, dim)


def halves(x):
    high = x.astype(BF16)
    return high, (x - high.astype(F32)).astype(BF16)


def dot(a, b):
    return jnp.dot(a, b, preferred_element_type=F32)


def dot_nt(a, b, precision=None):
    return lax.dot_general(
        a, b, (((1,), (1,)), ((), ())), preferred_element_type=F32, precision=precision
    )


def kernel(
    n,
    home_ref,
    tile_ref,
    table_ref,
    spread_hbm,
    sides_hbm,
    atmos_hbm,
    level_hbm,
    fuel_hbm,
    newlev_hbm,
    newatm_hbm,
    spread,
    sides,
    atmos,
    newatm,
    level,
    phi_a,
    phi_b,
    fuel,
    rate,
    reach,
    flow_r,
    flow_c,
    warm,
    acc,
    winds,
    patches,
    land,
    edge_a,
    rim_a,
    edge_b,
    rim_b,
    req,
    want,
    pick,
    back,
    heat,
    got,
    load_sem,
    save_sem,
    edge_send,
    rim_recv,
    all_send,
    all_recv,
):
    me = lax.axis_index("rows")
    slots = level.shape[0]
    pairs = slots // 2
    fields, levels, arows, ncols = atmos.shape
    strips = arows // CPT
    across = ncols // CPT
    cap = max(2, 2 * slots // n)
    nk = n * ROWS8

    loads = [
        pltpu.make_async_copy(src, dst, load_sem.at[i])
        for i, (src, dst) in enumerate(
            (
                (atmos_hbm, atmos),
                (fuel_hbm, fuel),
                (level_hbm, level),
                (spread_hbm, spread),
                (sides_hbm, sides),
            )
        )
    ]
    for load in loads:
        load.start()

    rim_a[...] = jnp.zeros_like(rim_a)
    rim_b[...] = jnp.zeros_like(rim_b)

    barrier = pltpu.get_barrier_semaphore()

    def greet(d, c):
        pl.semaphore_signal(
            barrier,
            inc=1,
            device_id={"rows": lax.rem(me + d, n)},
            device_id_type=pl.DeviceIdType.MESH,
        )
        return c

    lax.fori_loop(1, n, greet, 0)

    eye = iota((slots, slots), 0) == iota((slots, slots), 1)
    earlier = iota((slots, slots), 0) < iota((slots, slots), 1)
    home_row = home_ref[...].astype(F32)
    tile_row = tile_ref[...].astype(F32)
    home_col = jnp.sum(jnp.where(eye, home_row, 0.0), axis=1, keepdims=True)
    same = (home_col == home_row) & earlier
    rank_row = jnp.sum(jnp.where(same, 1.0, 0.0), axis=0, keepdims=True)
    place_row = home_row * ROWS8 + rank_row
    place_col = jnp.sum(jnp.where(eye, place_row, 0.0), axis=1, keepdims=True)
    placing_t = iota((nk, slots), 0).astype(F32) == place_row
    placing = jnp.where(place_col == iota((slots, nk), 1).astype(F32), 1.0, 0.0).astype(BF16)
    asked = jnp.sum(jnp.where(placing_t, tile_row, 0.0), axis=1, keepdims=True)
    req[...] = jnp.broadcast_to(asked, (nk, LANES))

    loads[0].wait()
    for side, row in ((0, arows - 1), (1, 0)):
        for f in range(2):
            edge_a[side, f : f + 1, :] = atmos[f, 0, row : row + 1, :]
        for f in range(fields):
            for k in range(levels):
                at = f * levels + k
                edge_b[side, at : at + 1, :] = atmos[f, k, row : row + 1, :]

    pl.semaphore_wait(barrier, n - 1)

    def edge_copy(side, which):
        src, dst = ((edge_a, rim_a), (edge_b, rim_b))[which]
        return pltpu.make_async_remote_copy(
            src_ref=src.at[side],
            dst_ref=dst.at[side],
            send_sem=edge_send.at[which, side],
            recv_sem=rim_recv.at[which, side],
            device_id={"rows": jnp.clip(me + (1 - 2 * side), 0, n - 1)},
            device_id_type=pl.DeviceIdType.MESH,
        )

    def send_edges(which):
        @pl.when(me < n - 1)
        def _():
            edge_copy(0, which).start()

        @pl.when(me > 0)
        def _():
            edge_copy(1, which).start()

    def recv_edges(which):
        @pl.when(me > 0)
        def _():
            edge_copy(0, which).wait_recv()

        @pl.when(me < n - 1)
        def _():
            edge_copy(1, which).wait_recv()

    def sent_edges(which):
        @pl.when(me < n - 1)
        def _():
            edge_copy(0, which).wait_send()

        @pl.when(me > 0)
        def _():
            edge_copy(1, which).wait_send()

    mine = pl.ds(pl.multiple_of(me * ROWS8, ROWS8), ROWS8)

    def exchange(src, dst, number):
        def send(d, c):
            peer = lax.rem(me + d, n)
            pltpu.make_async_remote_copy(
                src_ref=src.at[pl.ds(pl.multiple_of(peer * ROWS8, ROWS8), ROWS8)],
                dst_ref=dst.at[mine],
                send_sem=all_send.at[number],
                recv_sem=all_recv.at[number],
                device_id={"rows": peer},
                device_id_type=pl.DeviceIdType.MESH,
            ).start()
            return c

        lax.fori_loop(1, n, send, 0)

    def arrive(src, dst, number):
        others = pl.ds(0, (n - 1) * ROWS8)
        pltpu.make_async_copy(dst.at[others], dst.at[others], all_recv.at[number]).wait()
        dst[mine, :] = src[mine, :]

    def gone(src, number):
        others = pl.ds(0, (n - 1) * ROWS8)
        pltpu.make_async_copy(src.at[others], src.at[others], all_send.at[number]).wait()

    send_edges(0)
    exchange(req, want, 0)
    send_edges(1)

    loads[1].wait()

    low_half = iota((pairs, LANES), 1) < TILE

    def swap(x, y):
        turned_x = pltpu.roll(x, TILE, axis=1)
        turned_y = pltpu.roll(y, TILE, axis=1)
        return jnp.where(low_half, x, turned_y), jnp.where(low_half, turned_x, y)

    def narrow(v):
        return pl.ds(pl.multiple_of(v * LANES, LANES), LANES)

    def params(v, c):
        both = swap(fuel[:pairs, narrow(v)], fuel[pairs:, narrow(v)])
        for half in range(2):
            cols = narrow(2 * v + half)
            bits = [(both[half] & (1 << b)) != 0 for b in range(4)]
            for row, (ref, scale) in enumerate(
                ((rate, fire_step), (reach, fire_step), (warm, 1.0))
            ):
                vals = [table_ref[row, i] * scale for i in range(NFUEL)]
                for bit in bits:
                    vals = [
                        jnp.where(bit, vals[i + 1], vals[i]) if i + 1 < len(vals) else vals[i]
                        for i in range(0, len(vals), 2)
                    ]
                ref[:, cols] = vals[0]
            acc[:, cols] = jnp.zeros((pairs, LANES), F32)
        return c

    lax.fori_loop(0, CELLS // LANES, params, 0)

    recv_edges(0)
    for f in range(2):
        winds[f, 0:1, :] = rim_a[0, f : f + 1, :]
        winds[f, 1 : 1 + arows, :] = atmos[f, 0]
        winds[f, 1 + arows : 2 + arows, :] = rim_a[1, f : f + 1, :]
        winds[f, 2 + arows : 8 + arows, :] = jnp.zeros((6, ncols), F32)
    col8 = iota((ROWS8, ncols), 1)
    patches[...] = jnp.zeros_like(patches)
    for f in range(2):
        for strip in range(strips):
            base = winds[f, strip * CPT : strip * CPT + ROWS8, :]
            for q in range(SPAN):
                moved = base if q == 1 else pltpu.roll(base, (1 - q) % ncols, axis=1)
                if q == 0:
                    moved = jnp.where(col8 == 0, 0.0, moved)
                if q == SPAN - 1:
                    moved = jnp.where(col8 >= ncols - CPT, 0.0, moved)
                at = f * 64 + q * SPAN
                patches[at : at + SPAN, strip * ncols : (strip + 1) * ncols] = moved[:SPAN]
    table_high, table_low = halves(patches[...])

    arrive(req, want, 0)
    for chunk in range(0, nk, LANES):
        t = want[chunk : chunk + LANES, 0:1]
        hot = jnp.where(
            iota((LANES, strips * ncols), 1).astype(F32) == CPT * t, 1.0, 0.0
        ).astype(BF16)
        pick[chunk : chunk + LANES, :] = dot_nt(hot, table_high) + dot_nt(hot, table_low)
    exchange(pick, back, 1)

    for chunk in range(0, nk, LANES):
        t = want[chunk : chunk + LANES, 0:1]
        for strip in range(1, strips):
            t = jnp.where(t >= across, t - across, t)
        group = (iota((LANES, ncols), 1) // CPT).astype(F32)
        land[chunk : chunk + LANES, :] = jnp.where(group == t, 1.0, 0.0).astype(BF16)

    row8 = iota((arows, ncols), 0)
    colx = iota((arows, ncols), 1)
    def air(k):
        wind_r = atmos[0, k] * (0.5 * air_step)
        wind_c = atmos[1, k] * (0.5 * air_step)
        for f in range(fields):
            at = f * levels + k
            centre = atmos[f, k]
            north = jnp.where(row8 == 0, rim_b[0, at : at + 1, :], pltpu.roll(centre, 1, axis=0))
            south = jnp.where(
                row8 == arows - 1, rim_b[1, at : at + 1, :], pltpu.roll(centre, arows - 1, axis=0)
            )
            west = jnp.where(colx == 0, 0.0, pltpu.roll(centre, 1, axis=1))
            east = jnp.where(colx == ncols - 1, 0.0, pltpu.roll(centre, ncols - 1, axis=1))
            above = atmos[f, min(k + 1, levels - 1)]
            below = atmos[f, max(k - 1, 0)]
            laplace = north + south + west + east - 4.0 * centre
            vertical = above + below - 2.0 * centre
            carried = wind_r * (south - north) + wind_c * (east - west)
            newatm[f, k] = (
                centre
                + (air_step * viscosity) * laplace
                + (air_step * mixing) * vertical
                - carried
            )

    loads[2].wait()

    def pack(v, c):
        first, second = swap(level[:pairs, narrow(v)], level[pairs:, narrow(v)])
        phi_a[:, narrow(2 * v)] = first
        phi_a[:, narrow(2 * v + 1)] = second
        return c

    lax.fori_loop(0, CELLS // LANES, pack, 0)
    recv_edges(1)
    for k in range(levels // 2, levels):
        air(k)

    loads[3].wait()
    arrive(pick, back, 1)
    back_high, back_low = halves(back[...])
    own_high = dot(placing, back_high)
    own_low = dot(placing, back_low)
    lane = iota((slots, LANES), 1)
    ahead_parts = []
    for f in range(2):
        high, low = own_high, own_low
        if f:
            high, low = pltpu.roll(high, 64, axis=1), pltpu.roll(low, 64, axis=1)
        high, low = jnp.where(lane < PIECE, high, 0.0), jnp.where(lane < PIECE, low, 0.0)
        ahead_parts.append((high + pltpu.roll(low, PIECE, axis=1)).astype(BF16))
    left = jnp.concatenate(
        [jnp.concatenate([x[:pairs], x[pairs:]], axis=1) for x in ahead_parts], axis=0
    )
    along = dot(left, spread[...])
    table = weight_table()
    for f, ref in enumerate((flow_r, flow_c)):
        nodes = [along[f * pairs : (f + 1) * pairs, p * LANES : (p + 1) * LANES] for p in range(SPAN)]
        for a in range(TILE):
            cols = slice(a * LANES, (a + 1) * LANES)
            wind = sum(float(table[a, p]) * nodes[p] for p in range(SPAN) if table[a, p])
            ref[:, cols] = reach[:, cols] * wind

    loads[4].wait()
    sides_table = sides[...]
    batch = 8

    def substep(now, later):
        def row(i):
            return now[:, i * LANES : (i + 1) * LANES]

        for start in range(0, TILE, batch):
            split = [halves(row(i)) for i in range(start, start + batch)]
            parts = jnp.concatenate([jnp.concatenate(x, axis=1) for x in split], axis=0)
            across_cols = dot(parts, sides_table)
            centre = row(start)
            back_r = jnp.zeros_like(centre) if start == 0 else centre - row(start - 1)
            for i in range(start, start + batch):
                cols = slice(i * LANES, (i + 1) * LANES)
                here = slice((i - start) * pairs, (i - start + 1) * pairs)
                back_c = across_cols[here, :LANES]
                ahead_c = across_cols[here, LANES:]
                following = row(i + 1) if i + 1 < TILE else centre
                ahead_r = following - centre
                a = jnp.maximum(back_r, 0.0)
                b = jnp.minimum(ahead_r, 0.0)
                d = jnp.maximum(back_c, 0.0)
                e = jnp.minimum(ahead_c, 0.0)
                slope = (a * a + b * b) + (d * d + e * e) + spread_floor
                fr = flow_r[:, cols]
                fc = flow_c[:, cols]
                move = fr * jnp.where(fr > 0.0, back_r, ahead_r) + fc * jnp.where(
                    fc > 0.0, back_c, ahead_c
                )
                new = centre - (rate[:, cols] * (slope * lax.rsqrt(slope)) + move)
                later[:, cols] = new
                acc[:, cols] += jnp.exp(-(new * new))
                centre, back_r = following, ahead_r

    def two_substeps(pair, c):
        substep(phi_a, phi_b)
        substep(phi_b, phi_a)
        return c

    lax.fori_loop(0, SUBSTEPS // 2, two_substeps, 0)

    saves = [
        pltpu.make_async_copy(level, newlev_hbm, save_sem.at[0]),
        pltpu.make_async_copy(newatm, newatm_hbm, save_sem.at[1]),
    ]

    total = jnp.zeros((pairs, 2 * LANES), F32)
    for i in range(CPT):
        part = jnp.zeros((pairs, LANES), F32)
        for a in range(i * REFINE, (i + 1) * REFINE):
            cols = slice(a * LANES, (a + 1) * LANES)
            part = part + acc[:, cols] * warm[:, cols]
        source = iota((LANES, 2 * LANES), 0)
        target = iota((LANES, 2 * LANES), 1)
        spot = (source // TILE) * LANES + (source & (TILE - 1)) // REFINE + i * CPT
        mean = jnp.where(spot == target, 1.0 / (SUBSTEPS * REFINE * REFINE), 0.0).astype(BF16)
        part_high, part_low = halves(part)
        total = total + dot(part_high, mean) + dot(part_low, mean)
    total = jnp.concatenate([total[:, :LANES], total[:, LANES:]], axis=0)
    total_high, total_low = halves(total)
    out_of = jnp.where(placing_t, 1.0, 0.0).astype(BF16)
    heat[...] = dot(out_of, total_high) + dot(out_of, total_low)
    exchange(heat, got, 2)

    def unpack(v, c):
        first, second = swap(phi_a[:, narrow(2 * v)], phi_a[:, narrow(2 * v + 1)])
        level[:pairs, narrow(v)] = first
        level[pairs:, narrow(v)] = second
        return c

    lax.fori_loop(0, CELLS // LANES, unpack, 0)
    saves[0].start()
    for k in range(levels // 2):
        air(k)
    sent_edges(0)
    sent_edges(1)
    gone(req, 0)
    gone(pick, 1)
    arrive(heat, got, 2)

    spots = CPT * arows
    ranks = iota((spots, LANES), 0)
    r = ranks & (arows - 1)
    wanted_lane = (r // CPT) * (CPT * CPT) + (r % CPT) * CPT + ranks // arows
    choose = jnp.where(iota((spots, LANES), 1) == wanted_lane, 1.0, 0.0).astype(BF16)
    landed = jnp.zeros((2 * spots, ncols), F32)
    for chunk in range(0, nk, LANES):
        rows = slice(chunk, chunk + LANES)
        t = want[rows, :]
        x = got[rows, :]
        spread = jnp.zeros((LANES, LANES), F32)
        for strip in range(strips):
            here = (t >= strip * across) & (t < (strip + 1) * across)
            part = jnp.where(here, x, 0.0)
            if strip:
                part = pltpu.roll(part, strip * CPT * CPT, axis=1)
            spread = spread + part
        s_high, s_low = halves(spread)
        both = jnp.concatenate([dot_nt(choose, s_high), dot_nt(choose, s_low)], axis=0)
        landed = landed + dot(both.astype(BF16), land[rows, :])
    landed = landed[:spots] + landed[spots:]
    turn = colx & (CPT - 1)
    heating = landed[:arows]
    for j in range(1, CPT):
        heating = jnp.where(turn == j, landed[j * arows : (j + 1) * arows], heating)
    newatm[2, 0] = newatm[2, 0] + coupling * heating
    saves[1].start()
    gone(heat, 2)
    saves[0].wait()
    saves[1].wait()


def shards(n, atmos, level_set, fuel, fuel_table, band_home, band_tile):
    slots = level_set.shape[0]
    fields, levels, arows, ncols = atmos.shape
    nk = n * ROWS8
    cells = (slots, CELLS)
    packed = (slots // 2, 2 * CELLS)
    vmem = pltpu.VMEM
    hbm = pl.BlockSpec(memory_space=pl.ANY)
    local = pl.BlockSpec(memory_space=pltpu.VMEM)
    spread, sides = jnp.asarray(spread_weights()), jnp.asarray(side_weights())
    return pl.pallas_call(
        functools.partial(kernel, n),
        out_shape=(
            jax.ShapeDtypeStruct(level_set.shape, F32),
            jax.ShapeDtypeStruct(atmos.shape, F32),
        ),
        in_specs=[local, local, pl.BlockSpec(memory_space=pltpu.SMEM), hbm, hbm, hbm, hbm, hbm],
        out_specs=(hbm, hbm),
        scratch_shapes=[
            vmem(spread.shape, BF16),
            vmem(sides.shape, BF16),
            vmem(atmos.shape, F32),
            vmem(atmos.shape, F32),
            vmem(cells, F32),
            vmem(packed, F32),
            vmem(packed, F32),
            vmem(cells, jnp.int32),
        ]
        + [vmem(packed, F32)] * 6
        + [
            vmem((2, arows + 8, ncols), F32),
            vmem((LANES, arows // CPT * ncols), F32),
            vmem((nk, ncols), BF16),
            vmem((2, 2, ncols), F32),
            vmem((2, 2, ncols), F32),
            vmem((2, fields * levels, ncols), F32),
            vmem((2, fields * levels, ncols), F32),
        ]
        + [vmem((nk, LANES), F32)] * 6
        + [
            pltpu.SemaphoreType.DMA((5,)),
            pltpu.SemaphoreType.DMA((2,)),
            pltpu.SemaphoreType.DMA((2, 2)),
            pltpu.SemaphoreType.DMA((2, 2)),
            pltpu.SemaphoreType.DMA((3,)),
            pltpu.SemaphoreType.DMA((3,)),
        ],
        compiler_params=pltpu.CompilerParams(
            collective_id=0, has_side_effects=True, vmem_limit_bytes=62 * 1024 * 1024
        ),
    )(
        band_home.reshape(1, slots),
        band_tile.reshape(1, slots),
        fuel_table,
        spread,
        sides,
        atmos,
        level_set,
        fuel,
    )


def solution(mesh):
    placed = (
        P(None, None, ("groups", "rows"), None),
        P(("groups", "rows"), None),
        P(("groups", "rows"), None),
        P(),
        P(("groups", "rows"), None),
        P(("groups", "rows")),
    )
    return jax.shard_map(
        functools.partial(shards, mesh.shape["rows"]),
        mesh=mesh,
        in_specs=placed,
        out_specs=(P(("groups", "rows"), None), P(None, None, ("groups", "rows"), None)),
        check_vma=False,
    )
```
